512 devices in a mesh: yz: 128 (over z_lo, x, y, core), gx: 4 (over z_hi).
Axes of the slice: x: 4, y: 4, z: 16 (z_hi: 4, z_lo: 4; z = z_hi * 4 + z_lo), core: 2. Of those that a mesh axis runs over, the one named last changes fastest.
Arguments:
- state: float32 [7, 64, 1024, 128], P(None, 'gx', 'yz'), may hold values from -2.5 to 2.5
- register: float32 [7, 64, 1024, 128], P(None, 'gx', 'yz'), may hold values from -3 to 3
- forcing: float32 [3, 64, 1024, 128], P(None, 'gx', 'yz'), may hold values from -3 to 3
- y_shift: int32 [1], replicated, may hold values from 0 to 1023
Outputs:
- new_state: float32 [7, 64, 1024, 128], P(None, 'gx', 'yz')
- new_register: float32 [7, 64, 1024, 128], P(None, 'gx', 'yz')
The draws below stay inside these ranges and needn't reach their ends.
All inputs are finite; a program needn't handle non-finite values.
Results may differ from the reference program's by a relative error of at most 0.000092.
Values sent between devices are 32-bit elements; how exact they have to be, the bound alone decides.
A program may use at most 64 MiB of HBM per device.

```python
import jax
import jax.numpy as jnp
from jax import lax

NZ = 128
NX = 64
NY = 1024


def level_of(stream_key, extent, split, smallest, high):
    gain, own = 1.0, jax.random.fold_in(stream_key, 6)
    for position, shards_of in split:
        draws = jnp.exp(jax.random.uniform(jax.random.fold_in(own, position), (shards_of,), jnp.float32, smallest / len(split), high / len(split)))
        gain = gain * jnp.repeat(draws, extent[position] // shards_of).reshape([-1 if axis == position else 1 for axis in range(len(extent))])
    return gain


def bell_draw(own_key, extent, spread, limit, split=(), held_as=jnp.bfloat16):
    factor_of = level_of(own_key, extent, split, -0.22, 0.18) if split else 1.0
    drawn = jax.random.normal(own_key, extent, jnp.float32) * spread * factor_of
    return jnp.minimum(jnp.maximum(drawn, -limit), limit).astype(held_as)


def setup_inputs(seed: int = 0) -> dict:
    streams_of = jax.random.split(jax.random.key(seed), 5)
    return {
        "state": bell_draw(streams_of[0], (7, NX, NY, NZ), 0.4, 2.5, ((1, 4), (2, 128)), jnp.float32),
        "register": bell_draw(streams_of[1], (7, NX, NY, NZ), 0.5, 3.0, ((1, 4), (2, 128)), jnp.float32),
        "forcing": bell_draw(streams_of[2], (3, NX, NY, NZ), 0.5, 3.0, ((1, 4), (2, 128)), jnp.float32),
        "y_shift": jax.random.randint(streams_of[3], (1,), 0, NY).astype(jnp.int32),
    }


def first_diff(field, axis):
    count = field.shape[axis] - 6

    def part(offset):
        return lax.slice_in_dim(field, 3 + offset, 3 + offset + count, axis=axis)
    return (45.0 * (part(1) - part(-1)) - 9.0 * (part(2) - part(-2)) + (part(3) - part(-3))) / 60.0

def second_diff(field, axis):
    count = field.shape[axis] - 6

    def part(offset):
        return lax.slice_in_dim(field, 3 + offset, 3 + offset + count, axis=axis)
    return (-490.0 * part(0) + 270.0 * (part(1) + part(-1)) - 27.0 * (part(2) + part(-2)) + 2.0 * (part(3) + part(-3))) / 180.0

def inner(field, axes):
    for axis in axes:
        field = lax.slice_in_dim(field, 3, field.shape[axis] - 3, axis=axis)
    return field

def tendency(padded, forcing, xfrac, inv_width):
    grads = [inner(first_diff(padded, 1), (2, 3)), inner(first_diff(padded, 2), (1, 3)), inner(first_diff(padded, 3), (1, 2))]
    vectors = padded[:6]
    curv = [inner(second_diff(vectors, 1), (2, 3)), inner(second_diff(vectors, 2), (1, 3)), inner(second_diff(vectors, 3), (1, 2))]
    cross_xy = inner(first_diff(first_diff(vectors, 2), 1), (3,))
    cross_xz = inner(first_diff(first_diff(vectors, 3), 1), (2,))
    cross_yz = inner(first_diff(first_diff(vectors, 3), 2), (1,))
    center = inner(padded, (1, 2, 3))
    velx, vely, velz = (center[0], center[1], center[2])
    potx, poty = (center[3], center[4])

    def grad(axis, comp):
        return grads[axis][comp]

    def lapl(comp):
        return curv[0][comp] + curv[1][comp] + curv[2][comp]

    def grad_div(first):
        return (curv[0][first] + cross_xy[first + 1] + cross_xz[first + 2], cross_xy[first] + curv[1][first + 1] + cross_yz[first + 2], cross_xz[first] + cross_yz[first + 1] + curv[2][first + 2])
    fieldx = grad(1, 5) - grad(2, 4)
    fieldy = grad(2, 3) - grad(0, 5)
    fieldz = grad(0, 4) - grad(1, 3) + 0.5
    potdiv = grad_div(3)
    currx = potdiv[0] - lapl(3)
    curry = potdiv[1] - lapl(4)
    currz = potdiv[2] - lapl(5)
    veldiv = grad_div(0)
    inv_rho = jnp.exp(-center[6])
    flow = -1.5 * xfrac
    shear_rate = -1.5 * inv_width

    def advect(comp):
        return velx * grad(0, comp) + (vely + flow) * grad(1, comp) + velz * grad(2, comp)
    divu = grad(0, 0) + grad(1, 1) + grad(2, 2)

    def strain_term(row):
        total = jnp.zeros_like(velx)
        for col in range(3):
            strain = 0.5 * (grad(col, row) + grad(row, col))
            if col == row:
                strain = strain - divu / 3.0
            total = total + 2.0 * strain * grad(col, 6)
        return total
    lorentz = (curry * fieldz - currz * fieldy, currz * fieldx - currx * fieldz, currx * fieldy - curry * fieldx)
    emf = (vely * fieldz - velz * fieldy, velz * fieldx - velx * fieldz, velx * fieldy - vely * fieldx)
    curr = (currx, curry, currz)
    rates = []
    for comp in range(3):
        rate = -advect(comp) - grad(comp, 6) + lorentz[comp] * inv_rho
        rate = rate + 0.05 * (lapl(comp) + veldiv[comp] / 3.0 + strain_term(comp)) + forcing[comp]
        if comp == 0:
            rate = rate + 2.0 * 0.5 * vely
        if comp == 1:
            rate = rate - 2.0 * 0.5 * velx - shear_rate * velx
        rates.append(rate)
    for comp in range(3):
        rate = emf[comp] - flow * grad(1, 3 + comp) - 0.05 * curr[comp]
        if comp == 0:
            rate = rate - shear_rate * poty
        rates.append(rate)
    rates.append(-advect(6) - divu)
    return jnp.stack(rates)

def reference(state, register, forcing, y_shift):
    shift = y_shift[0]
    nx = state.shape[1]
    low = jnp.roll(state[:, nx - 3:], -shift, axis=2)
    high = jnp.roll(state[:, :3], shift, axis=2)
    ext = jnp.concatenate([low, state, high], axis=1)
    ext = jnp.concatenate([ext[:, :, -3:], ext, ext[:, :, :3]], axis=2)
    ext = jnp.concatenate([ext[:, :, :, -3:], ext, ext[:, :, :, :3]], axis=3)
    inv_width = 1.0 / nx
    width = 4
    starts = (jnp.arange(nx // width) * width).astype(jnp.int32)

    def block(start):
        piece = lax.dynamic_slice_in_dim(ext, start, width + 6, axis=1)
        push = lax.dynamic_slice_in_dim(forcing, start, width, axis=1)
        index = (start + jnp.arange(width)).astype(jnp.float32)
        xfrac = ((index + 0.5) * inv_width - 0.5).reshape(width, 1, 1)
        return tendency(piece, push, xfrac, inv_width)
    blocks = lax.map(block, starts)
    rate = jnp.transpose(blocks, (1, 0, 2, 3, 4)).reshape(state.shape)
    new_register = -5.0 / 9.0 * register + 0.15 * rate
    new_state = state + 15.0 / 16.0 * new_register
    return (new_state, new_register)
```

```python
import functools

import jax
import jax.numpy as jnp
from jax import lax
from jax.experimental import pallas as pl
from jax.experimental.pallas import tpu as pltpu
from jax.sharding import PartitionSpec as P

MESH = pl.DeviceIdType.MESH
ANY = pl.BlockSpec(memory_space=pl.ANY)
VMEM = pl.BlockSpec(memory_space=pltpu.VMEM)


def exchange(steps, slabs_x, slabs_y, state, out, send, recv, own):
    gx = lax.axis_index("gx")
    yz = lax.axis_index("yz")
    planes, rows = state.shape[1], state.shape[2]
    first = (gx == 0).astype(jnp.int32)
    last = (gx == slabs_x - 1).astype(jnp.int32)
    above = {"yz": lax.rem(yz + (slabs_y - steps) * last, slabs_y), "gx": lax.rem(gx + 1, slabs_x)}
    below = {"yz": lax.rem(yz + steps * first, slabs_y), "gx": lax.rem(gx + slabs_x - 1, slabs_x)}
    right = {"yz": lax.rem(yz + 1, slabs_y)}
    left = {"yz": lax.rem(yz + slabs_y - 1, slabs_y)}

    block = pltpu.make_async_copy(state, out.at[:, pl.ds(3, planes), pl.ds(rows, rows)], own)
    block.start()
    barrier = pltpu.get_barrier_semaphore()
    for peer in (above, below, right, left):
        pl.semaphore_signal(barrier, inc=1, device_id=peer, device_id_type=MESH)
    pl.semaphore_wait(barrier, 4)

    def copy(slot, source, target, peer):
        return pltpu.make_async_remote_copy(
            src_ref=source, dst_ref=target, send_sem=send.at[slot], recv_sem=recv.at[slot],
            device_id=peer, device_id_type=MESH)

    middle = pl.ds(rows, rows)
    low, high = pl.ds(0, 3), pl.ds(planes + 3, 3)
    ups = copy(0, state.at[:, pl.ds(planes - 3, 3)], out.at[:, low, middle], above)
    downs = copy(1, state.at[:, pl.ds(0, 3)], out.at[:, high, middle], below)
    ups.start()
    downs.start()
    inner = pl.ds(3, planes)
    rights = copy(2, state.at[:, :, pl.ds(rows - 3, 3)], out.at[:, inner, pl.ds(rows - 3, 3)], right)
    lefts = copy(3, state.at[:, :, pl.ds(0, 3)], out.at[:, inner, pl.ds(2 * rows, 3)], left)
    rights.start()
    lefts.start()
    later = []
    for k, (cross, at) in enumerate(((ups, low), (downs, high))):
        cross.wait_recv()
        for j, (target, peer) in enumerate(((0, right), (2 * rows, left))):
            c = copy(4 + 2 * k + j, out.at[:, at, middle], out.at[:, at, pl.ds(target, rows)], peer)
            c.start()
            later.append(c)
    ups.wait_send()
    downs.wait_send()
    rights.wait()
    lefts.wait()
    for c in later:
        c.wait()
    block.wait()


def extended(steps, slabs_x, slabs_y, state):
    fields, planes, rows, lanes = state.shape
    return pl.pallas_call(
        functools.partial(exchange, steps, slabs_x, slabs_y),
        out_shape=pltpu.VMEM((fields, planes + 6, 3 * rows, lanes), state.dtype),
        in_specs=[ANY],
        out_specs=VMEM,
        scratch_shapes=[
            pltpu.SemaphoreType.DMA((8,)),
            pltpu.SemaphoreType.DMA((8,)),
            pltpu.SemaphoreType.DMA,
        ],
        compiler_params=pltpu.CompilerParams(collective_id=steps, has_side_effects=True),
        name="extended",
    )(state)


def first_diff(low, high):
    return 0.75 * (high[0] - low[0]) - 0.15 * (high[1] - low[1]) + (1.0 / 60.0) * (high[2] - low[2])


def second_diff(center, *pairs):
    near, mid, far = (sum(high[k] + low[k] for low, high in pairs) for k in range(3))
    return (-490.0 / 180.0 * len(pairs)) * center + 1.5 * near - 0.15 * mid + (1.0 / 90.0) * far


def update(slabs_x, y_shift, ext, register, forcing, new_state, new_register, part):
    fields, planes, rows, lanes = new_state.shape
    gx = lax.axis_index("gx")
    offset = y_shift[0]
    left_over = lax.rem(offset + rows // 2, rows) - rows // 2

    def shear(at, by):
        for f in range(fields):
            for m in range(3):
                top = ext[f, at + m, pl.ds(rows - 3 + by, rows)]
                end = ext[f, at + m, pl.ds(rows + 3 + by, rows)]
                ext[f, at + m, pl.ds(rows - 3, rows)] = top
                ext[f, at + m, pl.ds(rows + 3, rows)] = end

    @pl.when(gx == 0)
    def _():
        shear(0, left_over)

    @pl.when(gx == slabs_x - 1)
    def _():
        shear(planes + 3, -left_over)

    def y_near(f, x):
        return tuple([ext[f, x, pl.ds(rows + sign * k, rows)] for k in (1, 2, 3)] for sign in (-1, 1))

    def x_near(f, x):
        return tuple([ext[f, x + sign * k, pl.ds(rows, rows)] for k in (1, 2, 3)] for sign in (-1, 1))

    def z_near(value):
        return (
            [pltpu.roll(value, k, 1) for k in (1, 2, 3)],
            [pltpu.roll(value, lanes - k, 1) for k in (1, 2, 3)],
        )

    def center(f, x):
        return ext[f, x, pl.ds(rows, rows)]

    def part_near(k, x):
        return tuple([part[k, x + sign * m] for m in (1, 2, 3)] for sign in (-1, 1))

    @pl.loop(0, planes + 6)
    def _(x):
        for k, f in ((0, 0), (3, 3)):
            dy = first_diff(*y_near(f + 1, x))
            dz = first_diff(*z_near(center(f + 2, x)))
            part[k, x] = first_diff(*y_near(f, x))
            part[k + 1, x] = dy
            part[k + 2, x] = dy + dz

    inv_width = 1.0 / (slabs_x * planes)
    shear_rate = -1.5 * inv_width

    @pl.loop(0, planes)
    def _(p):
        x = p + 3
        xfrac = ((gx * planes + p).astype(jnp.float32) + 0.5) * inv_width - 0.5
        flow = -1.5 * xfrac
        cen = [center(f, x) for f in range(fields)]
        nx = [x_near(f, x) for f in range(fields)]
        ny = [y_near(f, x) for f in range(fields)]
        nz = [z_near(cen[f]) for f in range(fields)]
        dx = [first_diff(*nx[f]) for f in range(fields)]
        dz = [first_diff(*nz[f]) for f in range(fields)]
        dy = [part[f, x] if f in (0, 1, 3, 4) else first_diff(*ny[f]) for f in range(fields)]
        sums = [first_diff(*part_near(k, x)) for k in (0, 2, 3, 5)]
        vel = cen[:3]
        carried = vel[1] + flow
        bx = dy[5] - dz[4]
        by = dz[3] - dx[5]
        bz = dx[4] - dy[3] + 0.5
        jx = sums[3] - second_diff(cen[3], ny[3], nz[3])
        jy = sums[2] + first_diff(*z_near(dy[5])) - second_diff(cen[4], nx[4], nz[4])
        jz = first_diff(*z_near(dx[3] + dy[4])) - second_diff(cen[5], nx[5], ny[5])
        curr = (jx, jy, jz)
        lorentz = (jy * bz - jz * by, jz * bx - jx * bz, jx * by - jy * bx)
        emf = (vel[1] * bz - vel[2] * by, vel[2] * bx - vel[0] * bz, vel[0] * by - vel[1] * bx)
        inv_rho = jnp.exp(-cen[6])
        divu = dx[0] + dy[1] + dz[2]
        rest = (
            sums[1],
            sums[0] + first_diff(*z_near(dy[2])),
            first_diff(*z_near(dx[0] + dy[1])),
        )
        grads = (dx, dy, dz)
        near = (nx, ny, nz)

        def advect(f):
            return vel[0] * dx[f] + carried * dy[f] + vel[2] * dz[f]

        rates = []
        for i in range(3):
            others = [near[a][i] for a in range(3) if a != i]
            viscous = second_diff(cen[i], *others) + (4.0 / 3.0) * second_diff(cen[i], near[i][i]) + rest[i] * (1.0 / 3.0)
            for j in range(3):
                if i == j:
                    strain = 2.0 * grads[i][i] - (2.0 / 3.0) * divu
                else:
                    strain = grads[j][i] + grads[i][j]
                viscous = viscous + strain * grads[j][6]
            rate = lorentz[i] * inv_rho - advect(i) - grads[i][6] + 0.05 * viscous + forcing[i, p]
            if i == 0:
                rate = rate + vel[1]
            if i == 1:
                rate = rate - (1.0 + shear_rate) * vel[0]
            rates.append(rate)
        for i in range(3):
            rate = emf[i] - flow * dy[3 + i] - 0.05 * curr[i]
            if i == 0:
                rate = rate - shear_rate * cen[4]
            rates.append(rate)
        rates.append(-advect(6) - divu)
        for f in range(fields):
            kept = (-5.0 / 9.0) * register[f, p] + 0.15 * rates[f]
            new_register[f, p] = kept
            new_state[f, p] = cen[f] + 0.9375 * kept


def per_device(state, register, forcing, y_shift):
    slabs_x = lax.axis_size("gx")
    slabs_y = lax.axis_size("yz")
    fields, planes, rows, lanes = state.shape
    whole = lax.div(y_shift[0] + rows // 2, rows)
    ext = lax.switch(
        lax.rem(whole, slabs_y),
        [functools.partial(extended, s, slabs_x, slabs_y) for s in range(slabs_y)],
        state,
    )
    ext = pltpu.with_memory_space_constraint(ext, pltpu.VMEM)
    return pl.pallas_call(
        functools.partial(update, slabs_x),
        out_shape=(jax.ShapeDtypeStruct(state.shape, state.dtype),) * 2,
        in_specs=[pl.BlockSpec(memory_space=pltpu.SMEM), VMEM, VMEM, VMEM],
        out_specs=(VMEM, VMEM),
        scratch_shapes=[pltpu.VMEM((6, planes + 6, rows, lanes), jnp.float32)],
        compiler_params=pltpu.CompilerParams(vmem_limit_bytes=40 * 2**20),
        name="update",
    )(y_shift, ext, register, forcing)


def solution(mesh):
    spec = P(None, "gx", "yz", None)
    return jax.shard_map(
        per_device,
        mesh=mesh,
        in_specs=(spec, spec, spec, P()),
        out_specs=(spec, spec),
        check_vma=False,
    )
```

```python
import functools

import jax
import jax.numpy as jnp
from jax import lax
from jax.experimental import pallas as pl
from jax.experimental.pallas import tpu as pltpu
from jax.sharding import PartitionSpec as P

MESH = pl.DeviceIdType.MESH
ANY = pl.BlockSpec(memory_space=pl.ANY)
VMEM = pl.BlockSpec(memory_space=pltpu.VMEM)


SPAN = 4
BACK = 12
SLOTS = 6
PARTS = ((0, 3), (3, 2), (5, 2))


def exchange(steps, slabs_x, slabs_y, state, out, ghost, send, recv, row_send, row_recv, far_send, far_recv, own, ready, near):
    gx = lax.axis_index("gx")
    yz = lax.axis_index("yz")
    planes, rows = state.shape[1], state.shape[2]
    first = (gx == 0).astype(jnp.int32)
    last = (gx == slabs_x - 1).astype(jnp.int32)
    above = {"yz": lax.rem(yz + (slabs_y - steps) * last, slabs_y), "gx": lax.rem(gx + 1, slabs_x)}
    below = {"yz": lax.rem(yz + steps * first, slabs_y), "gx": lax.rem(gx + slabs_x - 1, slabs_x)}

    def along(by):
        return {"yz": lax.rem(yz + (slabs_y + by), slabs_y)}

    def tell(semaphore, peer):
        pl.semaphore_signal(semaphore, inc=1, device_id=peer, device_id_type=MESH)

    def copy(source, target, send_sem, recv_sem, peer):
        return pltpu.make_async_remote_copy(
            src_ref=source, dst_ref=target, send_sem=send_sem, recv_sem=recv_sem,
            device_id=peer, device_id_type=MESH)

    block = pltpu.make_async_copy(state, out.at[:, pl.ds(3, planes), pl.ds(rows, rows)], own)

    def across(side, n):
        start, count = PARTS[n]
        source = state.at[pl.ds(start, count), pl.ds((planes - 3) * (1 - side), 3)]
        target = ghost.at[side, pl.ds(start, count), :, pl.ds((2 + side) * rows, rows)]
        return copy(source, target, far_send.at[side, n], far_recv.at[side, n], above if side == 0 else below)

    ups = [across(0, n) for n in range(len(PARTS))]
    downs = [across(1, n) for n in range(len(PARTS))]

    def start(copies):
        for c in copies:
            c.start()

    inner = pl.ds(3, planes)
    sides = [
        copy(state.at[:, :, pl.ds(rows - 3, 3)], out.at[:, inner, pl.ds(rows - 3, 3)], row_send.at[0], row_recv.at[0], along(1)),
        copy(state.at[:, :, pl.ds(0, 3)], out.at[:, inner, pl.ds(2 * rows, 3)], row_send.at[1], row_recv.at[1], along(-1)),
    ]

    barrier = pltpu.get_barrier_semaphore()
    far = slabs_x // 2
    tell(barrier, along(1))
    tell(barrier, along(-1))

    @pl.when((gx == 0) | (gx == 1))
    def _():
        tell(barrier, above)

    @pl.when((gx == 0) | (gx == slabs_x - 1))
    def _():
        tell(barrier, below)

    @pl.when(gx == 0)
    def _():
        pl.semaphore_wait(barrier, 2)
        start(sides)
        pl.semaphore_wait(ready.at[0], 1)
        start(ups)
        pl.semaphore_wait(ready.at[1], 1)
        start(downs)

    @pl.when(gx == 1)
    def _():
        pl.semaphore_wait(barrier, 3)
        start(downs)
        tell(ready.at[0], below)
        start(sides)
        pl.semaphore_wait(ready.at[0], 1)
        start(ups)

    @pl.when(gx == slabs_x - 1)
    def _():
        pl.semaphore_wait(barrier, 3)
        start(ups)
        tell(ready.at[1], above)
        start(sides)
        pl.semaphore_wait(ready.at[1], 1)
        start(downs)

    @pl.when(gx == far)
    def _():
        pl.semaphore_wait(barrier, 4)
        tell(ready.at[0], below)
        tell(ready.at[1], above)
        start(ups)
        start(downs)
        start(sides)

    block.start()
    edge = (gx == 0) | (gx == slabs_x - 1)

    @pl.when(edge)
    def _():
        for k in range(2):
            tell(near.at[k], along(1))
            tell(near.at[k], along(-1))
            pl.semaphore_wait(near.at[k], 2)

    def forward(side, n, k, by):
        begin, count = PARTS[n]
        fields = pl.ds(begin, count)
        own_rows = pl.ds(pl.multiple_of((2 + side) * rows, rows), rows)
        their_rows = pl.ds(pl.multiple_of((2 + side - by) * rows, rows), rows)
        return copy(
            ghost.at[side, fields, :, own_rows], ghost.at[side, fields, :, their_rows],
            send.at[side, n, k], recv.at[side, n, k], along(by))

    sooner = edge.astype(jnp.int32)
    passes = ((sooner, gx == slabs_x - 1), (1 - sooner, gx == 0))
    for side, sheared in passes:
        for n, (begin, count) in enumerate(PARTS):
            here = ghost.at[side, pl.ds(begin, count), :, pl.ds(pl.multiple_of((2 + side) * rows, rows), rows)]
            copy(here, here, far_send.at[side, n], far_recv.at[side, n], along(1)).wait_recv()
            for k, by in enumerate((1, -1)):
                forward(side, n, k, by).start()

            @pl.when(sheared)
            def _():
                for k, by in ((2, 2), (3, -2), (4, 6 * side - 3)):
                    forward(side, n, k, by).start()
    for c in ups + downs:
        c.wait_send()
    for c in sides:
        c.wait()
    for side, sheared in passes:
        for n in range(len(PARTS)):
            for k, by in enumerate((1, -1)):
                forward(side, n, k, by).wait()

            @pl.when(sheared)
            def _():
                for k, by in ((2, 2), (3, -2), (4, 6 * side - 3)):
                    forward(side, n, k, by).wait()
    block.wait()


def extended(steps, slabs_x, slabs_y, state):
    fields, planes, rows, lanes = state.shape
    parts = len(PARTS)
    dma = pltpu.SemaphoreType.DMA
    return pl.pallas_call(
        functools.partial(exchange, steps, slabs_x, slabs_y),
        out_shape=(
            pltpu.VMEM((fields, planes + 6, 3 * rows, lanes), state.dtype),
            pltpu.VMEM((2, fields, 3, SLOTS * rows, lanes), state.dtype),
        ),
        in_specs=[ANY],
        out_specs=(VMEM, VMEM),
        scratch_shapes=[
            dma((2, parts, 5)), dma((2, parts, 5)), dma((2,)), dma((2,)), dma((2, parts)), dma((2, parts)), dma,
            pltpu.SemaphoreType.REGULAR((2,)), pltpu.SemaphoreType.REGULAR((2,)),
        ],
        compiler_params=pltpu.CompilerParams(collective_id=steps // SPAN, has_side_effects=True),
        name="extended",
    )(state)


def first_diff(low, high):
    return 0.75 * (high[0] - low[0]) - 0.15 * (high[1] - low[1]) + (1.0 / 60.0) * (high[2] - low[2])


def second_diff(center, *pairs):
    near, mid, far = (sum(high[k] + low[k] for low, high in pairs) for k in range(3))
    return (-490.0 / 180.0 * len(pairs)) * center + 1.5 * near - 0.15 * mid + (1.0 / 90.0) * far


def update(slabs_x, y_shift, ghost, ext_in, register, forcing, new_state, new_register, ext, part):
    fields, planes, rows, lanes = new_state.shape
    gx = lax.axis_index("gx")
    left_over = lax.rem(y_shift[0] + BACK, SPAN * rows) - BACK
    by = (jnp.where(gx == 0, left_over, 0), jnp.where(gx == slabs_x - 1, -left_over, 0))
    for side in range(2):
        start = (2 + side) * rows + by[side]
        for f in range(fields):
            for m in range(3):
                at = side * (planes + 3) + m
                ext[f, at, pl.ds(rows - 3, rows)] = ghost[side, f, m, pl.ds(start - 3, rows)]
                ext[f, at, pl.ds(rows + 3, rows)] = ghost[side, f, m, pl.ds(start + 3, rows)]

    def y_near(f, x):
        return tuple([ext[f, x, pl.ds(rows + sign * k, rows)] for k in (1, 2, 3)] for sign in (-1, 1))

    def x_near(f, x):
        return tuple([ext[f, x + sign * k, pl.ds(rows, rows)] for k in (1, 2, 3)] for sign in (-1, 1))

    def z_near(value):
        return (
            [pltpu.roll(value, k, 1) for k in (1, 2, 3)],
            [pltpu.roll(value, lanes - k, 1) for k in (1, 2, 3)],
        )

    def center(f, x):
        return ext[f, x, pl.ds(rows, rows)]

    def part_near(k, x):
        return tuple([part[k, x + sign * m] for m in (1, 2, 3)] for sign in (-1, 1))

    @pl.loop(0, planes + 6)
    def _(x):
        for k, f in ((0, 0), (3, 3)):
            dy = first_diff(*y_near(f + 1, x))
            dz = first_diff(*z_near(center(f + 2, x)))
            part[k, x] = first_diff(*y_near(f, x))
            part[k + 1, x] = dy
            part[k + 2, x] = dy + dz

    inv_width = 1.0 / (slabs_x * planes)
    shear_rate = -1.5 * inv_width

    @pl.loop(0, planes)
    def _(p):
        x = p + 3
        xfrac = ((gx * planes + p).astype(jnp.float32) + 0.5) * inv_width - 0.5
        flow = -1.5 * xfrac
        cen = [center(f, x) for f in range(fields)]
        nx = [x_near(f, x) for f in range(fields)]
        ny = [y_near(f, x) for f in range(fields)]
        nz = [z_near(cen[f]) for f in range(fields)]
        dx = [first_diff(*nx[f]) for f in range(fields)]
        dz = [first_diff(*nz[f]) for f in range(fields)]
        dy = [part[f, x] if f in (0, 1, 3, 4) else first_diff(*ny[f]) for f in range(fields)]
        sums = [first_diff(*part_near(k, x)) for k in (0, 2, 3, 5)]
        vel = cen[:3]
        carried = vel[1] + flow
        bx = dy[5] - dz[4]
        by = dz[3] - dx[5]
        bz = dx[4] - dy[3] + 0.5
        jx = sums[3] - second_diff(cen[3], ny[3], nz[3])
        jy = sums[2] + first_diff(*z_near(dy[5])) - second_diff(cen[4], nx[4], nz[4])
        jz = first_diff(*z_near(dx[3] + dy[4])) - second_diff(cen[5], nx[5], ny[5])
        curr = (jx, jy, jz)
        lorentz = (jy * bz - jz * by, jz * bx - jx * bz, jx * by - jy * bx)
        emf = (vel[1] * bz - vel[2] * by, vel[2] * bx - vel[0] * bz, vel[0] * by - vel[1] * bx)
        inv_rho = jnp.exp(-cen[6])
        divu = dx[0] + dy[1] + dz[2]
        rest = (
            sums[1],
            sums[0] + first_diff(*z_near(dy[2])),
            first_diff(*z_near(dx[0] + dy[1])),
        )
        grads = (dx, dy, dz)
        near = (nx, ny, nz)

        def advect(f):
            return vel[0] * dx[f] + carried * dy[f] + vel[2] * dz[f]

        rates = []
        for i in range(3):
            others = [near[a][i] for a in range(3) if a != i]
            viscous = second_diff(cen[i], *others) + (4.0 / 3.0) * second_diff(cen[i], near[i][i]) + rest[i] * (1.0 / 3.0)
            for j in range(3):
                if i == j:
                    strain = 2.0 * grads[i][i] - (2.0 / 3.0) * divu
                else:
                    strain = grads[j][i] + grads[i][j]
                viscous = viscous + strain * grads[j][6]
            rate = lorentz[i] * inv_rho - advect(i) - grads[i][6] + 0.05 * viscous + forcing[i, p]
            if i == 0:
                rate = rate + vel[1]
            if i == 1:
                rate = rate - (1.0 + shear_rate) * vel[0]
            rates.append(rate)
        for i in range(3):
            rate = emf[i] - flow * dy[3 + i] - 0.05 * curr[i]
            if i == 0:
                rate = rate - shear_rate * cen[4]
            rates.append(rate)
        rates.append(-advect(6) - divu)
        for f in range(fields):
            kept = (-5.0 / 9.0) * register[f, p] + 0.15 * rates[f]
            new_register[f, p] = kept
            new_state[f, p] = cen[f] + 0.9375 * kept


def per_device(state, register, forcing, y_shift):
    slabs_x = lax.axis_size("gx")
    slabs_y = lax.axis_size("yz")
    fields, planes, rows, lanes = state.shape
    ext, ghost = lax.switch(
        lax.rem(lax.div(y_shift[0] + BACK, SPAN * rows), slabs_y // SPAN),
        [functools.partial(extended, s, slabs_x, slabs_y) for s in range(0, slabs_y, SPAN)],
        state,
    )
    ext = pltpu.with_memory_space_constraint(ext, pltpu.VMEM)
    ghost = pltpu.with_memory_space_constraint(ghost, pltpu.VMEM)
    new_state, new_register, _ = pl.pallas_call(
        functools.partial(update, slabs_x),
        out_shape=(jax.ShapeDtypeStruct(state.shape, state.dtype),) * 2 + (pltpu.VMEM(ext.shape, ext.dtype),),
        in_specs=[pl.BlockSpec(memory_space=pltpu.SMEM), VMEM, VMEM, VMEM, VMEM],
        out_specs=(VMEM, VMEM, VMEM),
        input_output_aliases={2: 2},
        scratch_shapes=[pltpu.VMEM((6, planes + 6, rows, lanes), jnp.float32)],
        compiler_params=pltpu.CompilerParams(vmem_limit_bytes=40 * 2**20),
        name="update",
    )(y_shift, ghost, ext, register, forcing)
    return new_state, new_register


def solution(mesh):
    spec = P(None, "gx", "yz", None)
    return jax.shard_map(
        per_device,
        mesh=mesh,
        in_specs=(spec, spec, spec, P()),
        out_specs=(spec, spec),
        check_vma=False,
    )
```

```python
import functools

import jax
import jax.numpy as jnp
from jax import lax
from jax.experimental import pallas as pl
from jax.experimental.pallas import tpu as pltpu
from jax.sharding import PartitionSpec as P

MESH = pl.DeviceIdType.MESH
ANY = pl.BlockSpec(memory_space=pl.ANY)
VMEM = pl.BlockSpec(memory_space=pltpu.VMEM)


SPAN = 4
BACK = 16
BASE = 3
SLOTS = 2 * BASE + 1
HALOED = 4


def exchange(
    steps, slabs_x, slabs_y, state, out, ghost, far_send, far_recv, row_send, row_recv, halo_send, halo_recv,
    shear_send, shear_recv, pass_recv, own, ready, near
):
    gx = lax.axis_index("gx")
    yz = lax.axis_index("yz")
    fields, planes, rows = state.shape[:3]
    first = (gx == 0).astype(jnp.int32)
    last = (gx == slabs_x - 1).astype(jnp.int32)
    above = {"yz": lax.rem(yz + (slabs_y - steps) * last, slabs_y), "gx": lax.rem(gx + 1, slabs_x)}
    below = {"yz": lax.rem(yz + steps * first, slabs_y), "gx": lax.rem(gx + slabs_x - 1, slabs_x)}
    core = lax.rem(yz, 2)
    twin = 1 - 2 * core

    def along(by):
        return {"yz": lax.rem(yz + (slabs_y + by), slabs_y)}

    def tell(semaphore, peer):
        pl.semaphore_signal(semaphore, inc=1, device_id=peer, device_id_type=MESH)

    def copy(source, target, send_sem, recv_sem, peer):
        return pltpu.make_async_remote_copy(
            src_ref=source, dst_ref=target, send_sem=send_sem, recv_sem=recv_sem,
            device_id=peer, device_id_type=MESH)

    every = pl.ds(0, fields)

    def one(field):
        return 0 if field is every else field

    def slot(side, field, at):
        return ghost.at[side, field, :, pl.ds(pl.multiple_of(at * rows, rows), rows)]

    def across(side, field):
        source = state.at[field, pl.ds((planes - 3) * (1 - side), 3)]
        return copy(source, slot(side, field, BASE), far_send.at[side], far_recv.at[side, one(field)], above if side == 0 else below)

    def cross(*sides):
        @pl.loop(0, fields)
        def _(field):
            for side in sides:
                across(side, field).start()

    inner = pl.ds(3, planes)
    beside = [
        copy(state.at[:, :, pl.ds(rows - 3, 3)], out.at[:, inner, pl.ds(rows - 3, 3)], row_send.at[0], row_recv.at[0], along(1)),
        copy(state.at[:, :, pl.ds(0, 3)], out.at[:, inner, pl.ds(2 * rows, 3)], row_send.at[1], row_recv.at[1], along(-1)),
    ]

    def trade():
        for c in beside:
            c.start()

    barrier = pltpu.get_barrier_semaphore()
    tell(barrier, along(1))
    tell(barrier, along(-1))

    @pl.when((gx == 0) | (gx == 1))
    def _():
        tell(barrier, above)

    @pl.when((gx == 0) | (gx == slabs_x - 1))
    def _():
        tell(barrier, below)

    @pl.when(gx == 0)
    def _():
        pl.semaphore_wait(barrier, 2)
        trade()
        pl.semaphore_wait(ready.at[0], 1)
        cross(0)
        pl.semaphore_wait(ready.at[1], 1)
        cross(1)

    @pl.when(gx == 1)
    def _():
        pl.semaphore_wait(barrier, 3)
        cross(1)
        tell(ready.at[0], below)
        trade()
        pl.semaphore_wait(ready.at[0], 1)
        cross(0)

    @pl.when(gx == slabs_x - 1)
    def _():
        pl.semaphore_wait(barrier, 3)
        cross(0)
        tell(ready.at[1], above)
        trade()
        pl.semaphore_wait(ready.at[1], 1)
        cross(1)

    @pl.when(gx == slabs_x // 2)
    def _():
        pl.semaphore_wait(barrier, 4)
        tell(ready.at[0], below)
        tell(ready.at[1], above)
        cross(0, 1)
        trade()

    block = pltpu.make_async_copy(state, out.at[:, inner, pl.ds(rows, rows)], own)
    block.start()
    edge = (gx == 0) | (gx == slabs_x - 1)

    @pl.when(edge)
    def _():
        for k in range(2):
            tell(near.at[k], along(1))
            tell(near.at[k], along(-1))
            pl.semaphore_wait(near.at[k], 2)

    def came(side, field):
        here = slot(side, field, BASE)
        copy(here, here, far_send.at[side], far_recv.at[side, field], along(1)).wait_recv()

    def rows_of(side, field, at, start):
        return ghost.at[side, field, :, pl.ds(at * rows + start, 3)]

    def halo(side, field, k):
        start, by = ((rows - 3, 1), (0, -1))[k]
        return copy(
            rows_of(side, field, BASE, start), rows_of(side, field, BASE - by, start),
            halo_send.at[side, k], halo_recv.at[side, k], along(by))

    def straight(side, field, k):
        by = (2, -2)[k]
        return copy(
            slot(side, field, BASE), slot(side, field, BASE - by), shear_send.at[k], pass_recv.at[k, one(field)], along(by))

    def to_twin(side, field, k):
        at = (BASE, BASE - 2, BASE + 2)[k]
        return copy(
            slot(side, field, at), slot(side, field, at - twin), shear_send.at[2 + k], shear_recv.at[k], along(twin))

    def corner(side, field, c):
        by, start = ((-3, 0), (3, rows - 3))[c]
        return copy(
            rows_of(side, field, BASE, start), rows_of(side, field, BASE - by, start),
            shear_send.at[5], shear_recv.at[3], along(by))

    def haloed(field):
        return (lax.rem(field, 3) != 2) & (field < 6)

    sooner = edge.astype(jnp.int32)
    for side, sheared in ((sooner, gx == slabs_x - 1), (1 - sooner, gx == 0)):

        @pl.when(jnp.logical_not(sheared))
        def _():
            @pl.loop(0, fields)
            def _(field):
                came(side, field)

                @pl.when(haloed(field))
                def _():
                    halo(side, field, 0).start()
                    halo(side, field, 1).start()

        @pl.when(sheared)
        def _():
            @pl.loop(0, fields)
            def _(field):
                came(side, field)
                straight(side, field, 0).start()
                straight(side, field, 1).start()
                to_twin(side, field, 0).start()
                for c in range(2):

                    @pl.when(haloed(field) & (core == c))
                    def _():
                        corner(side, field, c).start()

            @pl.loop(0, fields)
            def _(field):
                for k in range(2):
                    straight(side, field, k).wait_recv()
                    to_twin(side, field, 1 + k).start()

            for k in range(2):
                straight(side, every, k).wait_send()
            for k in range(3):
                to_twin(side, every, k).wait()
            corner(side, pl.ds(0, HALOED), 0).wait()

    for side in range(2):
        across(side, every).wait_send()

        @pl.when(gx != (slabs_x - 1) * side)
        def _():
            for k in range(2):
                halo(side, pl.ds(0, HALOED), k).wait()

    for c in beside:
        c.wait()
    block.wait()


def extended(steps, slabs_x, slabs_y, state):
    fields, planes, rows, lanes = state.shape
    dma, plain = pltpu.SemaphoreType.DMA, pltpu.SemaphoreType.REGULAR
    return pl.pallas_call(
        functools.partial(exchange, steps, slabs_x, slabs_y),
        out_shape=(
            pltpu.VMEM((fields, planes + 6, 3 * rows, lanes), state.dtype),
            pltpu.VMEM((2, fields, 3, SLOTS * rows, lanes), state.dtype),
        ),
        in_specs=[ANY],
        out_specs=(VMEM, VMEM),
        scratch_shapes=[
            dma((2,)), dma((2, fields)), dma((2,)), dma((2,)), dma((2, 2)), dma((2, 2)),
            dma((6,)), dma((4,)), dma((2, fields)), dma, plain((2,)), plain((2,)),
        ],
        compiler_params=pltpu.CompilerParams(
            collective_id=steps // SPAN, has_side_effects=True, vmem_limit_bytes=4 * 2**20
        ),
        name="extended",
    )(state)


def first_diff(low, high):
    return 0.75 * (high[0] - low[0]) - 0.15 * (high[1] - low[1]) + (1.0 / 60.0) * (high[2] - low[2])


def second_diff(center, *pairs):
    near, mid, far = (sum(high[k] + low[k] for low, high in pairs) for k in range(3))
    return (-490.0 / 180.0 * len(pairs)) * center + 1.5 * near - 0.15 * mid + (1.0 / 90.0) * far


def update(slabs_x, y_shift, ghost, ext_in, register, forcing, new_state, new_register, ext, part):
    fields, planes, rows, lanes = new_state.shape
    gx = lax.axis_index("gx")
    left_over = lax.rem(y_shift[0] + BACK, SPAN * rows) - BACK
    by = (jnp.where(gx == 0, left_over, 0), jnp.where(gx == slabs_x - 1, -left_over, 0))
    for side in range(2):
        start = BASE * rows + by[side]
        for f in range(fields):
            for m in range(3):
                at = side * (planes + 3) + m
                ext[f, at, pl.ds(rows - 3, rows)] = ghost[side, f, m, pl.ds(start - 3, rows)]
                ext[f, at, pl.ds(rows + 3, rows)] = ghost[side, f, m, pl.ds(start + 3, rows)]

    def y_near(f, x):
        return tuple([ext[f, x, pl.ds(rows + sign * k, rows)] for k in (1, 2, 3)] for sign in (-1, 1))

    def x_near(f, x):
        return tuple([ext[f, x + sign * k, pl.ds(rows, rows)] for k in (1, 2, 3)] for sign in (-1, 1))

    def z_near(value):
        return (
            [pltpu.roll(value, k, 1) for k in (1, 2, 3)],
            [pltpu.roll(value, lanes - k, 1) for k in (1, 2, 3)],
        )

    def center(f, x):
        return ext[f, x, pl.ds(rows, rows)]

    def part_near(k, x):
        return tuple([part[k, x + sign * m] for m in (1, 2, 3)] for sign in (-1, 1))

    @pl.loop(0, planes + 6, unroll=11)
    def _(x):
        for k, f in ((0, 0), (3, 3)):
            dy = first_diff(*y_near(f + 1, x))
            dz = first_diff(*z_near(center(f + 2, x)))
            part[k, x] = first_diff(*y_near(f, x))
            part[k + 1, x] = dy
            part[k + 2, x] = dy + dz

    inv_width = 1.0 / (slabs_x * planes)
    shear_rate = -1.5 * inv_width

    @pl.loop(0, planes, unroll=4)
    def _(p):
        x = p + 3
        xfrac = ((gx * planes + p).astype(jnp.float32) + 0.5) * inv_width - 0.5
        flow = -1.5 * xfrac
        cen = [center(f, x) for f in range(fields)]
        nx = [x_near(f, x) for f in range(fields)]
        ny = [y_near(f, x) for f in range(fields)]
        nz = [z_near(cen[f]) for f in range(fields)]
        dx = [first_diff(*nx[f]) for f in range(fields)]
        dz = [first_diff(*nz[f]) for f in range(fields)]
        dy = [part[f, x] if f in (0, 1, 3, 4) else first_diff(*ny[f]) for f in range(fields)]
        sums = [first_diff(*part_near(k, x)) for k in (0, 2, 3, 5)]
        vel = cen[:3]
        carried = vel[1] + flow
        bx = dy[5] - dz[4]
        by = dz[3] - dx[5]
        bz = dx[4] - dy[3] + 0.5
        jx = sums[3] - second_diff(cen[3], ny[3], nz[3])
        jy = sums[2] + first_diff(*z_near(dy[5])) - second_diff(cen[4], nx[4], nz[4])
        jz = first_diff(*z_near(dx[3] + dy[4])) - second_diff(cen[5], nx[5], ny[5])
        curr = (jx, jy, jz)
        lorentz = (jy * bz - jz * by, jz * bx - jx * bz, jx * by - jy * bx)
        emf = (vel[1] * bz - vel[2] * by, vel[2] * bx - vel[0] * bz, vel[0] * by - vel[1] * bx)
        inv_rho = jnp.exp(-cen[6])
        divu = dx[0] + dy[1] + dz[2]
        rest = (
            sums[1],
            sums[0] + first_diff(*z_near(dy[2])),
            first_diff(*z_near(dx[0] + dy[1])),
        )
        grads = (dx, dy, dz)
        near = (nx, ny, nz)

        def advect(f):
            return vel[0] * dx[f] + carried * dy[f] + vel[2] * dz[f]

        rates = []
        for i in range(3):
            others = [near[a][i] for a in range(3) if a != i]
            viscous = second_diff(cen[i], *others) + (4.0 / 3.0) * second_diff(cen[i], near[i][i]) + rest[i] * (1.0 / 3.0)
            for j in range(3):
                if i == j:
                    strain = 2.0 * grads[i][i] - (2.0 / 3.0) * divu
                else:
                    strain = grads[j][i] + grads[i][j]
                viscous = viscous + strain * grads[j][6]
            rate = lorentz[i] * inv_rho - advect(i) - grads[i][6] + 0.05 * viscous + forcing[i, p]
            if i == 0:
                rate = rate + vel[1]
            if i == 1:
                rate = rate - (1.0 + shear_rate) * vel[0]
            rates.append(rate)
        for i in range(3):
            rate = emf[i] - flow * dy[3 + i] - 0.05 * curr[i]
            if i == 0:
                rate = rate - shear_rate * cen[4]
            rates.append(rate)
        rates.append(-advect(6) - divu)
        for f in range(fields):
            kept = (-5.0 / 9.0) * register[f, p] + 0.15 * rates[f]
            new_register[f, p] = kept
            new_state[f, p] = cen[f] + 0.9375 * kept


def per_device(state, register, forcing, y_shift):
    slabs_x = lax.axis_size("gx")
    slabs_y = lax.axis_size("yz")
    fields, planes, rows, lanes = state.shape
    ext, ghost = lax.switch(
        lax.rem(lax.div(y_shift[0] + BACK, SPAN * rows), slabs_y // SPAN),
        [functools.partial(extended, s, slabs_x, slabs_y) for s in range(0, slabs_y, SPAN)],
        state,
    )
    ext = pltpu.with_memory_space_constraint(ext, pltpu.VMEM)
    ghost = pltpu.with_memory_space_constraint(ghost, pltpu.VMEM)
    new_state, new_register, _ = pl.pallas_call(
        functools.partial(update, slabs_x),
        out_shape=(jax.ShapeDtypeStruct(state.shape, state.dtype),) * 2 + (pltpu.VMEM(ext.shape, ext.dtype),),
        in_specs=[pl.BlockSpec(memory_space=pltpu.SMEM), VMEM, VMEM, VMEM, VMEM],
        out_specs=(VMEM, VMEM, VMEM),
        input_output_aliases={2: 2},
        scratch_shapes=[pltpu.VMEM((6, planes + 6, rows, lanes), jnp.float32)],
        compiler_params=pltpu.CompilerParams(vmem_limit_bytes=8 * 2**20),
        name="update",
    )(y_shift, ghost, ext, register, forcing)
    return new_state, new_register


def solution(mesh):
    spec = P(None, "gx", "yz", None)
    return jax.shard_map(
        per_device,
        mesh=mesh,
        in_specs=(spec, spec, spec, P()),
        out_specs=(spec, spec),
        check_vma=False,
    )
```

```python
import functools

import jax
import jax.numpy as jnp
from jax import lax
from jax.experimental import pallas as pl
from jax.experimental.pallas import tpu as pltpu
from jax.sharding import PartitionSpec as P

MESH = pl.DeviceIdType.MESH
ANY = pl.BlockSpec(memory_space=pl.ANY)
VMEM = pl.BlockSpec(memory_space=pltpu.VMEM)


SPAN = 4
BACK = 16
BASE = 3
SLOTS = 2 * BASE + 1
HALOED = 4


def exchange(
    steps, slabs_x, slabs_y, state, out, ghost, far_send, far_recv, row_send, row_recv, halo_send, halo_recv,
    shear_send, shear_recv, pass_recv, twice_send, own, ready, near
):
    gx = lax.axis_index("gx")
    yz = lax.axis_index("yz")
    fields, planes, rows = state.shape[:3]
    first = (gx == 0).astype(jnp.int32)
    last = (gx == slabs_x - 1).astype(jnp.int32)
    above = {"yz": lax.rem(yz + (slabs_y - steps) * last, slabs_y), "gx": lax.rem(gx + 1, slabs_x)}
    below = {"yz": lax.rem(yz + steps * first, slabs_y), "gx": lax.rem(gx + slabs_x - 1, slabs_x)}
    core = lax.rem(yz, 2)
    twin = 1 - 2 * core

    def along(by):
        return {"yz": lax.rem(yz + (slabs_y + by), slabs_y)}

    def tell(semaphore, peer):
        pl.semaphore_signal(semaphore, inc=1, device_id=peer, device_id_type=MESH)

    def copy(source, target, send_sem, recv_sem, peer):
        return pltpu.make_async_remote_copy(
            src_ref=source, dst_ref=target, send_sem=send_sem, recv_sem=recv_sem,
            device_id=peer, device_id_type=MESH)

    every = pl.ds(0, fields)

    def one(field):
        return 0 if field is every else field

    def slot(side, field, at):
        return ghost.at[side, field, :, pl.ds(pl.multiple_of(at * rows, rows), rows)]

    def across(side, field):
        source = state.at[field, pl.ds((planes - 3) * (1 - side), 3)]
        return copy(source, slot(side, field, BASE), far_send.at[side], far_recv.at[side, one(field)], above if side == 0 else below)

    def cross(*sides):
        @pl.loop(0, fields)
        def _(field):
            for side in sides:
                across(side, field).start()

    inner = pl.ds(3, planes)
    beside = [
        copy(state.at[:, :, pl.ds(rows - 3, 3)], out.at[:, inner, pl.ds(0, 3)], row_send.at[0], row_recv.at[0], along(1)),
        copy(state.at[:, :, pl.ds(0, 3)], out.at[:, inner, pl.ds(rows + 3, 3)], row_send.at[1], row_recv.at[1], along(-1)),
    ]

    def trade():
        for c in beside:
            c.start()

    ahead = lax.rem(yz + (slabs_y - steps), slabs_y)
    doubled = (gx == slabs_x - 1) & ((ahead < 2) | (ahead >= slabs_y - 2))
    spared = ((gx == 0) & (yz >= slabs_y - 2), (gx == 0) & (yz < 2))
    served = spared[0] | spared[1]

    def twice(field):
        downward = (ahead < 2).astype(jnp.int32)
        by = 2 - 4 * downward
        source = state.at[field, pl.ds(planes - 3, 3)]
        peer = {"yz": lax.rem(ahead + (slabs_y + by), slabs_y), "gx": lax.rem(gx + 1, slabs_x)}
        return copy(source, slot(0, field, BASE - by), twice_send, pass_recv.at[downward, one(field)], peer)

    barrier = pltpu.get_barrier_semaphore()
    tell(barrier, along(1))
    tell(barrier, along(-1))

    @pl.when((gx == 0) | (gx == 1))
    def _():
        tell(barrier, above)

    @pl.when((gx == 0) | (gx == slabs_x - 1))
    def _():
        tell(barrier, below)

    @pl.when(served)
    def _():
        over = 2 - 4 * (yz < 2).astype(jnp.int32)
        tell(barrier, {"yz": lax.rem(yz + (slabs_y + steps) + over, slabs_y), "gx": lax.rem(gx + slabs_x - 1, slabs_x)})

    @pl.when(gx == 0)
    def _():
        pl.semaphore_wait(barrier, 2)
        trade()
        pl.semaphore_wait(ready.at[0], 1)
        cross(0)
        pl.semaphore_wait(ready.at[1], 1)
        cross(1)

    @pl.when(gx == 1)
    def _():
        pl.semaphore_wait(barrier, 3)
        cross(1)
        tell(ready.at[0], below)
        trade()
        pl.semaphore_wait(ready.at[0], 1)
        cross(0)

    @pl.when(gx == slabs_x - 1)
    def _():
        pl.semaphore_wait(barrier, 3 + doubled.astype(jnp.int32))
        cross(0)
        tell(ready.at[1], above)

        @pl.when(doubled)
        def _():
            @pl.loop(0, fields)
            def _(field):
                twice(field).start()

        trade()
        pl.semaphore_wait(ready.at[1], 1)
        cross(1)

    @pl.when(gx == slabs_x // 2)
    def _():
        pl.semaphore_wait(barrier, 4)
        tell(ready.at[0], below)
        tell(ready.at[1], above)
        cross(0, 1)
        trade()

    block = pltpu.make_async_copy(state, out.at[:, inner, pl.ds(3, rows)], own)
    block.start()
    edge = (gx == 0) | (gx == slabs_x - 1)

    @pl.when(edge)
    def _():
        for k in range(2):
            tell(near.at[k], along(1))
            tell(near.at[k], along(-1))
            pl.semaphore_wait(near.at[k], 2)

    def came(side, field):
        here = slot(side, field, BASE)
        copy(here, here, far_send.at[side], far_recv.at[side, field], along(1)).wait_recv()

    def rows_of(side, field, at, start):
        return ghost.at[side, field, :, pl.ds(at * rows + start, 3)]

    def halo(side, field, k):
        start, by = ((rows - 3, 1), (0, -1))[k]
        return copy(
            rows_of(side, field, BASE, start), rows_of(side, field, BASE - by, start),
            halo_send.at[side, k], halo_recv.at[side, k], along(by))

    def straight(side, field, k):
        by = (2, -2)[k]
        return copy(
            slot(side, field, BASE), slot(side, field, BASE - by), shear_send.at[k], pass_recv.at[k, one(field)], along(by))

    def to_twin(side, field, k):
        at = (BASE, BASE - 2, BASE + 2)[k]
        return copy(
            slot(side, field, at), slot(side, field, at - twin), shear_send.at[2 + k], shear_recv.at[k], along(twin))

    def corner(side, field, c):
        by, start = ((-3, 0), (3, rows - 3))[c]
        return copy(
            rows_of(side, field, BASE, start), rows_of(side, field, BASE - by, start),
            shear_send.at[5], shear_recv.at[3], along(by))

    def haloed(field):
        return (lax.rem(field, 3) != 2) & (field < 6)

    def halos(side):
        @pl.loop(0, fields)
        def _(field):
            came(side, field)

            @pl.when(haloed(field))
            def _():
                halo(side, field, 0).start()
                halo(side, field, 1).start()

    def sheared(side):
        @pl.loop(0, fields)
        def _(field):
            came(side, field)
            to_twin(side, field, 0).start()
            for k in range(2):

                @pl.when(jnp.logical_not(spared[k]))
                def _():
                    straight(side, field, k).start()

            for c in range(2):

                @pl.when(haloed(field) & (core == c))
                def _():
                    corner(side, field, c).start()

        @pl.loop(0, fields)
        def _(field):
            for k in range(2):
                straight(side, field, k).wait_recv()
                to_twin(side, field, 1 + k).start()

        for k in range(2):

            @pl.when(jnp.logical_not(spared[k]))
            def _():
                straight(side, every, k).wait_send()

        for k in range(3):
            to_twin(side, every, k).wait()
        corner(side, pl.ds(0, HALOED), 0).wait()

    halos(first)

    @pl.when(jnp.logical_not(edge))
    def _():
        halos(1 - first)

    @pl.when(edge)
    def _():
        sheared(1 - first)

    for side in range(2):
        across(side, every).wait_send()

        @pl.when(gx != (slabs_x - 1) * side)
        def _():
            for k in range(2):
                halo(side, pl.ds(0, HALOED), k).wait()

    @pl.when(doubled)
    def _():
        twice(every).wait_send()

    for c in beside:
        c.wait()
    block.wait()


def extended(steps, slabs_x, slabs_y, state):
    fields, planes, rows, lanes = state.shape
    dma, plain = pltpu.SemaphoreType.DMA, pltpu.SemaphoreType.REGULAR
    return pl.pallas_call(
        functools.partial(exchange, steps, slabs_x, slabs_y),
        out_shape=(
            pltpu.VMEM((fields, planes + 6, 2 * rows, lanes), state.dtype),
            pltpu.VMEM((2, fields, 3, SLOTS * rows, lanes), state.dtype),
        ),
        in_specs=[ANY],
        out_specs=(VMEM, VMEM),
        scratch_shapes=[
            dma((2,)), dma((2, fields)), dma((2,)), dma((2,)), dma((2, 2)), dma((2, 2)),
            dma((6,)), dma((4,)), dma((2, fields)), dma, dma, plain((2,)), plain((2,)),
        ],
        compiler_params=pltpu.CompilerParams(
            collective_id=steps // SPAN, has_side_effects=True, vmem_limit_bytes=4 * 2**20
        ),
        name="extended",
    )(state)


def first_diff(low, high):
    return 0.75 * (high[0] - low[0]) - 0.15 * (high[1] - low[1]) + (1.0 / 60.0) * (high[2] - low[2])


def second_diff(center, *pairs):
    near, mid, far = (sum(high[k] + low[k] for low, high in pairs) for k in range(3))
    return (-490.0 / 180.0 * len(pairs)) * center + 1.5 * near - 0.15 * mid + (1.0 / 90.0) * far


def update(slabs_x, y_shift, ghost, ext_in, register, forcing, new_state, new_register, ext, part):
    fields, planes, rows, lanes = new_state.shape
    gx = lax.axis_index("gx")
    left_over = lax.rem(y_shift[0] + BACK, SPAN * rows) - BACK
    by = (jnp.where(gx == 0, left_over, 0), jnp.where(gx == slabs_x - 1, -left_over, 0))
    for side in range(2):
        start = BASE * rows + by[side]
        for f in range(fields):
            for m in range(3):
                at = side * (planes + 3) + m
                ext[f, at, pl.ds(0, rows)] = ghost[side, f, m, pl.ds(start - 3, rows)]
                ext[f, at, pl.ds(rows, rows)] = ghost[side, f, m, pl.ds(start + rows - 3, rows)]

    def y_near(f, x):
        return tuple([ext[f, x, pl.ds(3 + sign * k, rows)] for k in (1, 2, 3)] for sign in (-1, 1))

    def x_near(f, x):
        return tuple([ext[f, x + sign * k, pl.ds(3, rows)] for k in (1, 2, 3)] for sign in (-1, 1))

    def z_near(value):
        return (
            [pltpu.roll(value, k, 1) for k in (1, 2, 3)],
            [pltpu.roll(value, lanes - k, 1) for k in (1, 2, 3)],
        )

    def center(f, x):
        return ext[f, x, pl.ds(3, rows)]

    def part_near(k, x):
        return tuple([part[k, x + sign * m] for m in (1, 2, 3)] for sign in (-1, 1))

    @pl.loop(0, planes + 6, unroll=11)
    def _(x):
        for k, f in ((0, 0), (3, 3)):
            dy = first_diff(*y_near(f + 1, x))
            dz = first_diff(*z_near(center(f + 2, x)))
            part[k, x] = first_diff(*y_near(f, x))
            part[k + 1, x] = dy
            part[k + 2, x] = dy + dz

    inv_width = 1.0 / (slabs_x * planes)
    shear_rate = -1.5 * inv_width

    @pl.loop(0, planes, unroll=4)
    def _(p):
        x = p + 3
        xfrac = ((gx * planes + p).astype(jnp.float32) + 0.5) * inv_width - 0.5
        flow = -1.5 * xfrac
        cen = [center(f, x) for f in range(fields)]
        nx = [x_near(f, x) for f in range(fields)]
        ny = [y_near(f, x) for f in range(fields)]
        nz = [z_near(cen[f]) for f in range(fields)]
        dx = [first_diff(*nx[f]) for f in range(fields)]
        dz = [first_diff(*nz[f]) for f in range(fields)]
        dy = [part[f, x] if f in (0, 1, 3, 4) else first_diff(*ny[f]) for f in range(fields)]
        sums = [first_diff(*part_near(k, x)) for k in (0, 2, 3, 5)]
        vel = cen[:3]
        carried = vel[1] + flow
        bx = dy[5] - dz[4]
        by = dz[3] - dx[5]
        bz = dx[4] - dy[3] + 0.5
        jx = sums[3] - second_diff(cen[3], ny[3], nz[3])
        jy = sums[2] + first_diff(*z_near(dy[5])) - second_diff(cen[4], nx[4], nz[4])
        jz = first_diff(*z_near(dx[3] + dy[4])) - second_diff(cen[5], nx[5], ny[5])
        curr = (jx, jy, jz)
        lorentz = (jy * bz - jz * by, jz * bx - jx * bz, jx * by - jy * bx)
        emf = (vel[1] * bz - vel[2] * by, vel[2] * bx - vel[0] * bz, vel[0] * by - vel[1] * bx)
        inv_rho = jnp.exp(-cen[6])
        divu = dx[0] + dy[1] + dz[2]
        rest = (
            sums[1],
            sums[0] + first_diff(*z_near(dy[2])),
            first_diff(*z_near(dx[0] + dy[1])),
        )
        grads = (dx, dy, dz)
        near = (nx, ny, nz)

        def advect(f):
            return vel[0] * dx[f] + carried * dy[f] + vel[2] * dz[f]

        rates = []
        for i in range(3):
            others = [near[a][i] for a in range(3) if a != i]
            viscous = second_diff(cen[i], *others) + (4.0 / 3.0) * second_diff(cen[i], near[i][i]) + rest[i] * (1.0 / 3.0)
            for j in range(3):
                if i == j:
                    strain = 2.0 * grads[i][i] - (2.0 / 3.0) * divu
                else:
                    strain = grads[j][i] + grads[i][j]
                viscous = viscous + strain * grads[j][6]
            rate = lorentz[i] * inv_rho - advect(i) - grads[i][6] + 0.05 * viscous + forcing[i, p]
            if i == 0:
                rate = rate + vel[1]
            if i == 1:
                rate = rate - (1.0 + shear_rate) * vel[0]
            rates.append(rate)
        for i in range(3):
            rate = emf[i] - flow * dy[3 + i] - 0.05 * curr[i]
            if i == 0:
                rate = rate - shear_rate * cen[4]
            rates.append(rate)
        rates.append(-advect(6) - divu)
        for f in range(fields):
            kept = (-5.0 / 9.0) * register[f, p] + 0.15 * rates[f]
            new_register[f, p] = kept
            new_state[f, p] = cen[f] + 0.9375 * kept


def per_device(state, register, forcing, y_shift):
    slabs_x = lax.axis_size("gx")
    slabs_y = lax.axis_size("yz")
    fields, planes, rows, lanes = state.shape
    ext, ghost = lax.switch(
        lax.rem(lax.div(y_shift[0] + BACK, SPAN * rows), slabs_y // SPAN),
        [functools.partial(extended, s, slabs_x, slabs_y) for s in range(0, slabs_y, SPAN)],
        state,
    )
    ext = pltpu.with_memory_space_constraint(ext, pltpu.VMEM)
    ghost = pltpu.with_memory_space_constraint(ghost, pltpu.VMEM)
    new_state, new_register, _ = pl.pallas_call(
        functools.partial(update, slabs_x),
        out_shape=(jax.ShapeDtypeStruct(state.shape, state.dtype),) * 2 + (pltpu.VMEM(ext.shape, ext.dtype),),
        in_specs=[pl.BlockSpec(memory_space=pltpu.SMEM), VMEM, VMEM, VMEM, VMEM],
        out_specs=(VMEM, VMEM, VMEM),
        input_output_aliases={2: 2},
        scratch_shapes=[pltpu.VMEM((6, planes + 6, rows, lanes), jnp.float32)],
        compiler_params=pltpu.CompilerParams(vmem_limit_bytes=8 * 2**20),
        name="update",
    )(y_shift, ghost, ext, register, forcing)
    return new_state, new_register


def solution(mesh):
    spec = P(None, "gx", "yz", None)
    return jax.shard_map(
        per_device,
        mesh=mesh,
        in_specs=(spec, spec, spec, P()),
        out_specs=(spec, spec),
        check_vma=False,
    )
```

```python
import functools

import jax
import jax.numpy as jnp
from jax import lax
from jax.experimental import pallas as pl
from jax.experimental.pallas import tpu as pltpu
from jax.sharding import PartitionSpec as P

MESH = pl.DeviceIdType.MESH
ANY = pl.BlockSpec(memory_space=pl.ANY)
VMEM = pl.BlockSpec(memory_space=pltpu.VMEM)


SPAN = 4
BACK = 16
BASE = 3
SLOTS = 2 * BASE + 1
HALOED = 4


def exchange(
    steps, slabs_x, slabs_y, state, out, ghost, far_send, far_recv, row_send, row_recv, halo_send, halo_recv,
    shear_send, shear_recv, pass_recv, twice_send, own, ready, near
):
    gx = lax.axis_index("gx")
    yz = lax.axis_index("yz")
    fields, planes, rows = state.shape[:3]
    first = (gx == 0).astype(jnp.int32)
    last = (gx == slabs_x - 1).astype(jnp.int32)
    above = {"yz": lax.rem(yz + (slabs_y - steps) * last, slabs_y), "gx": lax.rem(gx + 1, slabs_x)}
    below = {"yz": lax.rem(yz + steps * first, slabs_y), "gx": lax.rem(gx + slabs_x - 1, slabs_x)}
    core = lax.rem(yz, 2)
    twin = 1 - 2 * core

    def along(by):
        return {"yz": lax.rem(yz + (slabs_y + by), slabs_y)}

    def tell(semaphore, peer):
        pl.semaphore_signal(semaphore, inc=1, device_id=peer, device_id_type=MESH)

    def copy(source, target, send_sem, recv_sem, peer):
        return pltpu.make_async_remote_copy(
            src_ref=source, dst_ref=target, send_sem=send_sem, recv_sem=recv_sem,
            device_id=peer, device_id_type=MESH)

    every = pl.ds(0, fields)

    def one(field):
        return 0 if field is every else field

    def slot(side, field, at):
        return ghost.at[side, field, :, pl.ds(pl.multiple_of(at * rows, rows), rows)]

    def across(side, field):
        source = state.at[field, pl.ds((planes - 3) * (1 - side), 3)]
        return copy(source, slot(side, field, BASE), far_send.at[side], far_recv.at[side, one(field)], above if side == 0 else below)

    def cross(*sides):
        @pl.loop(0, fields)
        def _(field):
            for side in sides:
                across(side, field).start()

    inner = pl.ds(3, planes)
    beside = [
        copy(state.at[:, :, pl.ds(rows - 3, 3)], out.at[:, inner, pl.ds(0, 3)], row_send.at[0], row_recv.at[0], along(1)),
        copy(state.at[:, :, pl.ds(0, 3)], out.at[:, inner, pl.ds(rows + 3, 3)], row_send.at[1], row_recv.at[1], along(-1)),
    ]

    def trade():
        for c in beside:
            c.start()

    ahead = lax.rem(yz + (slabs_y - steps), slabs_y)
    doubled = (gx == slabs_x - 1) & ((ahead < 2) | (ahead >= slabs_y - 2))
    spared = ((gx == 0) & (yz >= slabs_y - 2), (gx == 0) & (yz < 2))
    served = spared[0] | spared[1]

    def twice(field):
        downward = (ahead < 2).astype(jnp.int32)
        by = 2 - 4 * downward
        source = state.at[field, pl.ds(planes - 3, 3)]
        peer = {"yz": lax.rem(ahead + (slabs_y + by), slabs_y), "gx": lax.rem(gx + 1, slabs_x)}
        return copy(source, slot(0, field, BASE - by), twice_send, pass_recv.at[downward, one(field)], peer)

    def hail(k):
        tell(near.at[k], along(1))
        tell(near.at[k], along(-1))

    barrier = pltpu.get_barrier_semaphore()
    tell(barrier, along(1))
    tell(barrier, along(-1))

    @pl.when((gx == 0) | (gx == 1))
    def _():
        tell(barrier, above)

    @pl.when((gx == 0) | (gx == slabs_x - 1))
    def _():
        tell(barrier, below)

    @pl.when(served)
    def _():
        over = 2 - 4 * (yz < 2).astype(jnp.int32)
        tell(barrier, {"yz": lax.rem(yz + (slabs_y + steps) + over, slabs_y), "gx": lax.rem(gx + slabs_x - 1, slabs_x)})

    @pl.when(gx == 0)
    def _():
        pl.semaphore_wait(barrier, 2)
        hail(0)
        trade()
        pl.semaphore_wait(ready.at[0], 1)
        cross(0)
        pl.semaphore_wait(near.at[0], 2)
        hail(1)
        pl.semaphore_wait(ready.at[1], 1)
        cross(1)

    @pl.when(gx == 1)
    def _():
        pl.semaphore_wait(barrier, 3)
        cross(1)
        tell(ready.at[0], below)
        trade()
        pl.semaphore_wait(ready.at[0], 1)
        cross(0)

    @pl.when(gx == slabs_x - 1)
    def _():
        pl.semaphore_wait(barrier, 3 + doubled.astype(jnp.int32))
        cross(0)
        tell(ready.at[1], above)

        @pl.when(doubled)
        def _():
            @pl.loop(0, fields)
            def _(field):
                twice(field).start()

        hail(0)
        trade()
        pl.semaphore_wait(near.at[0], 2)
        hail(1)
        pl.semaphore_wait(ready.at[1], 1)
        cross(1)

    @pl.when(gx == slabs_x // 2)
    def _():
        pl.semaphore_wait(barrier, 4)
        tell(ready.at[0], below)
        tell(ready.at[1], above)
        cross(0, 1)
        trade()

    block = pltpu.make_async_copy(state, out.at[:, inner, pl.ds(3, rows)], own)
    block.start()
    edge = (gx == 0) | (gx == slabs_x - 1)

    @pl.when(edge)
    def _():
        pl.semaphore_wait(near.at[1], 2)

    def came(side, field):
        here = slot(side, field, BASE)
        copy(here, here, far_send.at[side], far_recv.at[side, field], along(1)).wait_recv()

    def rows_of(side, field, at, start):
        return ghost.at[side, field, :, pl.ds(at * rows + start, 3)]

    def halo(side, field, k):
        start, by = ((rows - 3, 1), (0, -1))[k]
        return copy(
            rows_of(side, field, BASE, start), rows_of(side, field, BASE - by, start),
            halo_send.at[side, k], halo_recv.at[side, k], along(by))

    def straight(side, field, k):
        by = (2, -2)[k]
        return copy(
            slot(side, field, BASE), slot(side, field, BASE - by), shear_send.at[k], pass_recv.at[k, one(field)], along(by))

    def to_twin(side, field, k):
        at = (BASE, BASE - 2, BASE + 2)[k]
        return copy(
            slot(side, field, at), slot(side, field, at - twin), shear_send.at[2 + k], shear_recv.at[k], along(twin))

    def corner(side, field, c):
        by, start = ((-3, 0), (3, rows - 3))[c]
        return copy(
            rows_of(side, field, BASE, start), rows_of(side, field, BASE - by, start),
            shear_send.at[5], shear_recv.at[3], along(by))

    def haloed(field):
        return (lax.rem(field, 3) != 2) & (field < 6)

    def halos(side):
        @pl.loop(0, fields)
        def _(field):
            came(side, field)

            @pl.when(haloed(field))
            def _():
                halo(side, field, 0).start()
                halo(side, field, 1).start()

    def sheared(side):
        @pl.loop(0, fields)
        def _(field):
            came(side, field)
            to_twin(side, field, 0).start()
            for k in range(2):

                @pl.when(jnp.logical_not(spared[k]))
                def _():
                    straight(side, field, k).start()

            for c in range(2):

                @pl.when(haloed(field) & (core == c))
                def _():
                    corner(side, field, c).start()

        @pl.loop(0, fields)
        def _(field):
            for k in range(2):
                straight(side, field, k).wait_recv()
                to_twin(side, field, 1 + k).start()

        for k in range(2):

            @pl.when(jnp.logical_not(spared[k]))
            def _():
                straight(side, every, k).wait_send()

        for k in range(3):
            to_twin(side, every, k).wait()
        corner(side, pl.ds(0, HALOED), 0).wait()

    halos(first)

    @pl.when(jnp.logical_not(edge))
    def _():
        halos(1 - first)

    @pl.when(edge)
    def _():
        sheared(1 - first)

    for side in range(2):
        across(side, every).wait_send()

        @pl.when(gx != (slabs_x - 1) * side)
        def _():
            for k in range(2):
                halo(side, pl.ds(0, HALOED), k).wait()

    @pl.when(doubled)
    def _():
        twice(every).wait_send()

    for c in beside:
        c.wait()
    block.wait()


def extended(steps, slabs_x, slabs_y, state):
    fields, planes, rows, lanes = state.shape
    dma, plain = pltpu.SemaphoreType.DMA, pltpu.SemaphoreType.REGULAR
    return pl.pallas_call(
        functools.partial(exchange, steps, slabs_x, slabs_y),
        out_shape=(
            pltpu.VMEM((fields, planes + 6, 2 * rows, lanes), state.dtype),
            pltpu.VMEM((2, fields, 3, SLOTS * rows, lanes), state.dtype),
        ),
        in_specs=[ANY],
        out_specs=(VMEM, VMEM),
        scratch_shapes=[
            dma((2,)), dma((2, fields)), dma((2,)), dma((2,)), dma((2, 2)), dma((2, 2)),
            dma((6,)), dma((4,)), dma((2, fields)), dma, dma, plain((2,)), plain((2,)),
        ],
        compiler_params=pltpu.CompilerParams(
            collective_id=steps // SPAN, has_side_effects=True, vmem_limit_bytes=4 * 2**20
        ),
        name="extended",
    )(state)


def first_diff(low, high):
    return 0.75 * (high[0] - low[0]) - 0.15 * (high[1] - low[1]) + (1.0 / 60.0) * (high[2] - low[2])


def second_diff(center, *pairs):
    near, mid, far = (sum(high[k] + low[k] for low, high in pairs) for k in range(3))
    return (-490.0 / 180.0 * len(pairs)) * center + 1.5 * near - 0.15 * mid + (1.0 / 90.0) * far


def update(slabs_x, y_shift, ghost, ext_in, register, forcing, new_state, new_register, ext, part):
    fields, planes, rows, lanes = new_state.shape
    gx = lax.axis_index("gx")
    left_over = lax.rem(y_shift[0] + BACK, SPAN * rows) - BACK
    by = (jnp.where(gx == 0, left_over, 0), jnp.where(gx == slabs_x - 1, -left_over, 0))
    for side in range(2):
        start = BASE * rows + by[side]
        for f in range(fields):
            for m in range(3):
                at = side * (planes + 3) + m
                ext[f, at, pl.ds(0, rows)] = ghost[side, f, m, pl.ds(start - 3, rows)]
                ext[f, at, pl.ds(rows, rows)] = ghost[side, f, m, pl.ds(start + rows - 3, rows)]

    def y_near(f, x):
        return tuple([ext[f, x, pl.ds(3 + sign * k, rows)] for k in (1, 2, 3)] for sign in (-1, 1))

    def x_near(f, x):
        return tuple([ext[f, x + sign * k, pl.ds(3, rows)] for k in (1, 2, 3)] for sign in (-1, 1))

    def z_near(value):
        return (
            [pltpu.roll(value, k, 1) for k in (1, 2, 3)],
            [pltpu.roll(value, lanes - k, 1) for k in (1, 2, 3)],
        )

    def center(f, x):
        return ext[f, x, pl.ds(3, rows)]

    def part_near(k, x):
        return tuple([part[k, x + sign * m] for m in (1, 2, 3)] for sign in (-1, 1))

    @pl.loop(0, planes + 6, unroll=11)
    def _(x):
        for k, f in ((0, 0), (3, 3)):
            dy = first_diff(*y_near(f + 1, x))
            dz = first_diff(*z_near(center(f + 2, x)))
            part[k, x] = first_diff(*y_near(f, x))
            part[k + 1, x] = dy
            part[k + 2, x] = dy + dz

    inv_width = 1.0 / (slabs_x * planes)
    shear_rate = -1.5 * inv_width

    @pl.loop(0, planes, unroll=4)
    def _(p):
        x = p + 3
        xfrac = ((gx * planes + p).astype(jnp.float32) + 0.5) * inv_width - 0.5
        flow = -1.5 * xfrac
        cen = [center(f, x) for f in range(fields)]
        nx = [x_near(f, x) for f in range(fields)]
        ny = [y_near(f, x) for f in range(fields)]
        nz = [z_near(cen[f]) for f in range(fields)]
        dx = [first_diff(*nx[f]) for f in range(fields)]
        dz = [first_diff(*nz[f]) for f in range(fields)]
        dy = [part[f, x] if f in (0, 1, 3, 4) else first_diff(*ny[f]) for f in range(fields)]
        sums = [first_diff(*part_near(k, x)) for k in (0, 2, 3, 5)]
        vel = cen[:3]
        carried = vel[1] + flow
        bx = dy[5] - dz[4]
        by = dz[3] - dx[5]
        bz = dx[4] - dy[3] + 0.5
        jx = sums[3] - second_diff(cen[3], ny[3], nz[3])
        jy = sums[2] + first_diff(*z_near(dy[5])) - second_diff(cen[4], nx[4], nz[4])
        jz = first_diff(*z_near(dx[3] + dy[4])) - second_diff(cen[5], nx[5], ny[5])
        curr = (jx, jy, jz)
        lorentz = (jy * bz - jz * by, jz * bx - jx * bz, jx * by - jy * bx)
        emf = (vel[1] * bz - vel[2] * by, vel[2] * bx - vel[0] * bz, vel[0] * by - vel[1] * bx)
        inv_rho = jnp.exp(-cen[6])
        divu = dx[0] + dy[1] + dz[2]
        rest = (
            sums[1],
            sums[0] + first_diff(*z_near(dy[2])),
            first_diff(*z_near(dx[0] + dy[1])),
        )
        grads = (dx, dy, dz)
        near = (nx, ny, nz)

        def advect(f):
            return vel[0] * dx[f] + carried * dy[f] + vel[2] * dz[f]

        rates = []
        for i in range(3):
            others = [near[a][i] for a in range(3) if a != i]
            viscous = second_diff(cen[i], *others) + (4.0 / 3.0) * second_diff(cen[i], near[i][i]) + rest[i] * (1.0 / 3.0)
            for j in range(3):
                if i == j:
                    strain = 2.0 * grads[i][i] - (2.0 / 3.0) * divu
                else:
                    strain = grads[j][i] + grads[i][j]
                viscous = viscous + strain * grads[j][6]
            rate = lorentz[i] * inv_rho - advect(i) - grads[i][6] + 0.05 * viscous + forcing[i, p]
            if i == 0:
                rate = rate + vel[1]
            if i == 1:
                rate = rate - (1.0 + shear_rate) * vel[0]
            rates.append(rate)
        for i in range(3):
            rate = emf[i] - flow * dy[3 + i] - 0.05 * curr[i]
            if i == 0:
                rate = rate - shear_rate * cen[4]
            rates.append(rate)
        rates.append(-advect(6) - divu)
        for f in range(fields):
            kept = (-5.0 / 9.0) * register[f, p] + 0.15 * rates[f]
            new_register[f, p] = kept
            new_state[f, p] = cen[f] + 0.9375 * kept


def per_device(state, register, forcing, y_shift):
    slabs_x = lax.axis_size("gx")
    slabs_y = lax.axis_size("yz")
    fields, planes, rows, lanes = state.shape
    ext, ghost = lax.switch(
        lax.rem(lax.div(y_shift[0] + BACK, SPAN * rows), slabs_y // SPAN),
        [functools.partial(extended, s, slabs_x, slabs_y) for s in range(0, slabs_y, SPAN)],
        state,
    )
    ext = pltpu.with_memory_space_constraint(ext, pltpu.VMEM)
    ghost = pltpu.with_memory_space_constraint(ghost, pltpu.VMEM)
    new_state, new_register, _ = pl.pallas_call(
        functools.partial(update, slabs_x),
        out_shape=(jax.ShapeDtypeStruct(state.shape, state.dtype),) * 2 + (pltpu.VMEM(ext.shape, ext.dtype),),
        in_specs=[pl.BlockSpec(memory_space=pltpu.SMEM), VMEM, VMEM, VMEM, VMEM],
        out_specs=(VMEM, VMEM, VMEM),
        input_output_aliases={2: 2},
        scratch_shapes=[pltpu.VMEM((6, planes + 6, rows, lanes), jnp.float32)],
        compiler_params=pltpu.CompilerParams(vmem_limit_bytes=8 * 2**20),
        name="update",
    )(y_shift, ghost, ext, register, forcing)
    return new_state, new_register


def solution(mesh):
    spec = P(None, "gx", "yz", None)
    return jax.shard_map(
        per_device,
        mesh=mesh,
        in_specs=(spec, spec, spec, P()),
        out_specs=(spec, spec),
        check_vma=False,
    )
```
